1024 devices in a mesh: row: 16 (over x_lo, z), col: 64 (over y, x_hi, core).
Axes of the slice: x: 8 (x_hi: 4, x_lo: 2; x = x_hi * 2 + x_lo), y: 8, z: 8, core: 2. Of those that a mesh axis runs over, the one named last changes fastest.
Arguments:
- base_weights: float32 [32, 7168, 2048], P(None, 'col', 'row'), may hold values from -6 to 6
- factor_down: float32 [32, 7168, 128], P(None, 'col', 'row'), may hold values from -6 to 6
- factor_up: float32 [32, 128, 2048], P(None, 'col', 'row'), may hold values from -0.5 to 0.5
- presence: int32 [2, 16], replicated, may hold values 0 or 1
- serving_order: int32 [32], replicated, may hold values from 0 to 31, each once
Outputs:
- served: bfloat16 [32, 7168, 2048], P('row', 'col')
The draws below stay inside these ranges and needn't reach their ends.
Inputs may be any that keep to these rules, and one draw needn't show every extreme that they name: `serving_order`: each value appears exactly once.
All inputs are finite; a program needn't handle non-finite values.
Results may differ from the reference program's by a relative error of at most 0.00105.
Values may be sent and summed in bfloat16 or wider, within the bound.
No kernel may reach another device: no remote copies, remote signals or barrier semaphores. Data moves between devices by JAX's collectives and lax.ppermute only.
A program may use at most 32 MiB of HBM per device.

```python
import jax
import jax.numpy as jnp
from jax import lax

D = 7168
FF = 2048
RANK = 128
LAYERS = 2
EXP_L = 16
EXPERTS = 32


def set_ends(values, stream_key, least, high):
    longest = values.shape.index(max(values.shape))
    spots = []
    for shift in (0, 1):
        where = [jax.random.randint(jax.random.fold_in(stream_key, axis), (), 0, length) for axis, length in enumerate(values.shape)]
        where[longest] = (where[longest] + shift) % values.shape[longest]
        spots.append(tuple(where))
    return values.at[spots[0]].set(least).at[spots[1]].set(high)


def block_scale(own_key, extent, pieces, least, top_value):
    def one(axis_at, parts):
        heights = jax.random.uniform(jax.random.fold_in(jax.random.fold_in(own_key, 6), axis_at), (parts,), jnp.float32, least / len(pieces), top_value / len(pieces))
        return jnp.repeat(jnp.exp(heights), extent[axis_at] // parts).reshape((-1,) + (1,) * (len(extent) - axis_at - 1))

    level = one(*pieces[0])
    for cut in pieces[1:]:
        level = level * one(*cut)
    return level


def bell_draw(stream_key, extent, width, bound, shards=(), held_as=jnp.bfloat16):
    values = width * jax.random.normal(stream_key, extent, jnp.float32)
    if shards:
        values = values * block_scale(stream_key, extent, shards, -0.22, 0.18)
    return jnp.clip(values, -bound, bound).astype(held_as)


def setup_inputs(seed: int = 0) -> dict:
    arg_keys = jax.random.split(jax.random.key(seed), 6)
    base_weights = bell_draw(arg_keys[0], (EXPERTS, D, FF), 1.0, 6.0, ((1, 64), (2, 16)), jnp.float32)
    factor_down = bell_draw(arg_keys[1], (EXPERTS, D, RANK), 1.0, 6.0, ((1, 64), (2, 16)), jnp.float32)
    factor_up = bell_draw(arg_keys[2], (EXPERTS, RANK, FF), RANK ** -0.5, 0.5, ((1, 64), (2, 16)), jnp.float32)
    presence = set_ends((jax.random.randint(arg_keys[3], (LAYERS, EXP_L), 0, 4) < 3).astype(jnp.int32), jax.random.fold_in(arg_keys[3], 1), 0, 1)
    serving_order = jax.random.permutation(arg_keys[4], EXPERTS).astype(jnp.int32)
    return {"base_weights": base_weights, "factor_down": factor_down, "factor_up": factor_up, "presence": presence, "serving_order": serving_order}


def reference(base_weights, factor_down, factor_up, presence, serving_order):
    flags = presence.reshape(EXPERTS).astype(jnp.float32)

    def one_expert(index):
        delta = jnp.dot(factor_down[index], factor_up[index], precision=lax.Precision.HIGHEST, preferred_element_type=jnp.float32)
        return (base_weights[index] + flags[index] * delta).astype(jnp.bfloat16)

    return lax.map(one_expert, serving_order.astype(jnp.int32))
```

```python
import functools

import jax
import jax.numpy as jnp
from jax import lax
from jax.experimental import pallas as pl
from jax.experimental.pallas import tpu as pltpu
from jax.sharding import Mesh, PartitionSpec as P

TOP = 32767.0
BASE_MAX = 6.0
DOWN_MAX = 6.0
UP_MAX = 0.5
PAIRS = 16
ROWS = 112
TILE = 128
RANKS = 8
FF = 2048


def code_of(most, bound):
    root = jnp.sqrt(jnp.sqrt(most * (1.0 / bound)))
    return jnp.clip(jnp.ceil(root * TOP), 1.0, TOP)


def step_of(code, bound):
    part = code * (1.0 / TOP)
    part = part * part
    return part * part * (bound / TOP)


def coded(values, code, bound):
    return jnp.clip(jnp.round(values / step_of(code, bound)), -TOP, TOP)


def to16(values):
    return values.astype(jnp.int32).astype(jnp.int16)


def pack_kernel(per, order_ref, base_ref, down_ref, up_ref, out_ref, up_rows):
    first = pl.program_id(0) * per
    row8 = lax.broadcasted_iota(jnp.int32, (8, TILE), 0)
    lane = lax.broadcasted_iota(jnp.int32, (8, TILE), 1)
    up_rows[...] = jnp.zeros_like(up_rows)
    for p in range(per):
        downs, base_codes = [], []
        for e in range(2):
            expert = order_ref[(first + p) * 2 + e]
            tile = base_ref[expert]
            code = code_of(jnp.max(jnp.abs(tile), axis=0, keepdims=True), BASE_MAX)
            inverse = 1.0 / step_of(code, BASE_MAX)
            out_ref[p, e, 0:ROWS, :] = to16(jnp.clip(jnp.round(tile * inverse), -TOP, TOP))
            base_codes.append(code)
            factor = down_ref[expert]
            most = jnp.max(jnp.abs(factor), axis=1, keepdims=True)
            code = code_of(jnp.broadcast_to(most, (RANKS, TILE)), DOWN_MAX)
            wide = jnp.concatenate([factor, jnp.zeros((RANKS, TILE - ROWS), jnp.float32)], axis=1)
            downs.append(jnp.where(lane < ROWS, coded(wide, code, DOWN_MAX), code))
            up_rows[2 * e : 2 * e + 2, :] = up_ref[expert]
        low = (row8 & 2) == 0
        own = jnp.where(low, downs[0], pltpu.roll(downs[1], 2, 0))
        other = jnp.where(low, pltpu.roll(downs[0], 6, 0), downs[1])
        out_ref[p, 0, ROWS:TILE, :] = to16(jnp.concatenate([own, other], axis=0))
        ups = up_rows[...]
        most = jnp.max(jnp.abs(ups), axis=1, keepdims=True)
        code = code_of(jnp.broadcast_to(most, (8, TILE)), UP_MAX)
        head = jnp.where(row8 < 4, coded(ups, code, UP_MAX), pltpu.roll(code, 4, 0))
        tail = jnp.where(row8 == 0, base_codes[0], jnp.where(row8 == 1, base_codes[1], 0.0))
        out_ref[p, 1, ROWS:TILE, :] = to16(jnp.concatenate([head, tail], axis=0))


def pack(order, base, down, up):
    per = 4
    return pl.pallas_call(
        functools.partial(pack_kernel, per),
        grid_spec=pltpu.PrefetchScalarGridSpec(
            num_scalar_prefetch=1,
            grid=(PAIRS // per,),
            in_specs=[
                pl.BlockSpec(base.shape, lambda i, o: (0, 0, 0)),
                pl.BlockSpec(down.shape, lambda i, o: (0, 0, 0)),
                pl.BlockSpec(up.shape, lambda i, o: (0, 0, 0)),
            ],
            out_specs=pl.BlockSpec((per, 2, TILE, TILE), lambda i, o: (i, 0, 0, 0)),
            scratch_shapes=[pltpu.VMEM((8, TILE), jnp.float32)],
        ),
        out_shape=jax.ShapeDtypeStruct((PAIRS, 2, TILE, TILE), jnp.int16),
        compiler_params=pltpu.CompilerParams(vmem_limit_bytes=24 * 2**20),
        cost_estimate=pl.CostEstimate(flops=4_000_000, bytes_accessed=3_000_000, transcendentals=0),
    )(order, base, down, up)


def merge_kernel(per, order_ref, flag_ref, place_ref, tile_ref, down_ref, own_ref, other_ref, own_code, other_code, out_ref, left_hi, left_lo):
    row, core = place_ref[0], place_ref[1]

    @pl.when(pl.program_id(0) == 0)
    def _():
        flags = [flag_ref[order_ref[2 * row + e]].astype(jnp.float32) for e in range(2)]
        rows = down_ref[:, 0, :, :].astype(jnp.float32)
        halves = [rows[:, 0:8, :].reshape(TILE, TILE), rows[:, 8:16, :].reshape(TILE, TILE)]
        mine = jnp.where(core == 0, halves[0], halves[1])
        theirs = jnp.where(core == 0, halves[1], halves[0])
        expert = (lax.broadcasted_iota(jnp.int32, (TILE, TILE), 0) >> 1) & 1
        for h, (factor, code_ref) in enumerate(((mine, own_code), (theirs, other_code))):
            scale = step_of(factor[:, ROWS : ROWS + 1], DOWN_MAX) * step_of(code_ref[...].astype(jnp.float32), UP_MAX)
            factor = factor * scale
            for e in range(2):
                part = jnp.where(expert == e, factor * flags[e], 0.0).T[0:ROWS, :]
                high = part.astype(jnp.bfloat16)
                left_hi[e * ROWS : (e + 1) * ROWS, h * TILE : (h + 1) * TILE] = high
                left_lo[e * ROWS : (e + 1) * ROWS, h * TILE : (h + 1) * TILE] = (part - high.astype(jnp.float32)).astype(jnp.bfloat16)

    right = jnp.concatenate([own_ref[...], other_ref[...]], axis=0).astype(jnp.float32)
    high = right.astype(jnp.bfloat16)
    low = (right - high.astype(jnp.float32)).astype(jnp.bfloat16)
    dot = functools.partial(jnp.dot, preferred_element_type=jnp.float32)
    delta = dot(left_hi[...], high) + (dot(left_lo[...], high) + dot(left_hi[...], low))
    for s in range(per):
        codes = tile_ref[s, 1, ROWS:TILE, :].astype(jnp.float32)
        for e in range(2):
            base = tile_ref[s, e, 0:ROWS, :].astype(jnp.float32) * step_of(codes[8 + e : 9 + e, :], BASE_MAX)
            total = base + delta[e * ROWS : (e + 1) * ROWS, s * TILE : (s + 1) * TILE]
            out_ref[e, :, s * TILE : (s + 1) * TILE] = total.astype(jnp.bfloat16)


def merge(order, flags, place, tiles, own, other):
    per = 4
    wide = per * TILE
    last = FF // TILE
    half = pl.BlockSpec((TILE, wide), lambda i, *_: (0, i))
    code = pl.BlockSpec((TILE, TILE), lambda i, *_: (0, last))
    return pl.pallas_call(
        functools.partial(merge_kernel, per),
        grid_spec=pltpu.PrefetchScalarGridSpec(
            num_scalar_prefetch=3,
            grid=(PAIRS // per,),
            in_specs=[
                pl.BlockSpec((per, 2, TILE, TILE), lambda i, *_: (i, 0, 0, 0)),
                pl.BlockSpec((PAIRS, 1, 16, TILE), lambda i, *_: (0, 0, ROWS // 16, 0)),
                half,
                half,
                code,
                code,
            ],
            out_specs=pl.BlockSpec((2, ROWS, wide), lambda i, *_: (0, 0, i)),
            scratch_shapes=[pltpu.VMEM((2 * ROWS, 2 * TILE), jnp.bfloat16)] * 2,
        ),
        out_shape=jax.ShapeDtypeStruct((2, ROWS, FF), jnp.bfloat16),
        compiler_params=pltpu.CompilerParams(vmem_limit_bytes=24 * 2**20),
        cost_estimate=pl.CostEstimate(flops=700_000_000, bytes_accessed=4_000_000, transcendentals=0),
    )(order, flags, place, tiles, tiles, own, other, own, other)


def body(base_weights, factor_down, factor_up, presence, serving_order):
    place = jnp.stack([lax.axis_index("row"), lax.axis_index("core")]).astype(jnp.int32)
    sent = pack(serving_order, base_weights, jnp.swapaxes(factor_down, 1, 2), factor_up)
    tiles = lax.all_to_all(sent, "row", split_axis=0, concat_axis=0, tiled=True)

    rows = tiles[:, 1, ROWS : ROWS + 8, :].astype(jnp.float32)
    codes = rows[:, 4:8]
    most = jnp.max(codes, axis=0)
    ratio = codes / most
    ratio = ratio * ratio
    ups = jnp.clip(jnp.round(rows[:, 0:4] * (ratio * ratio)), -TOP, TOP)
    ups = jnp.concatenate([ups, most[None]], axis=0).astype(jnp.int16)
    ups = jnp.transpose(ups, (1, 0, 2)).reshape(4, FF + TILE)
    own = lax.all_to_all(jnp.broadcast_to(ups[None], (32,) + ups.shape), ("y", "xh"), split_axis=0, concat_axis=0, tiled=True)
    own = own.reshape(TILE, FF + TILE)
    other = lax.ppermute(own, "core", [(0, 1), (1, 0)])
    return merge(serving_order, presence.reshape(-1), place, tiles, own, other)


def solution(mesh):
    fine = Mesh(mesh.devices.reshape(16, 8, 4, 2), ("row", "y", "xh", "core"))
    col = ("y", "xh", "core")
    return jax.shard_map(
        body,
        mesh=fine,
        in_specs=(P(None, col, "row"), P(None, col, "row"), P(None, col, "row"), P(), P()),
        out_specs=P("row", col, None),
        check_vma=False,
    )
```

```python
import functools

import jax
import jax.numpy as jnp
from jax import lax
from jax.experimental import pallas as pl
from jax.experimental.pallas import tpu as pltpu
from jax.sharding import Mesh, PartitionSpec as P

TOP = 32767.0
BASE_MAX = 6.0
DOWN_MAX = 6.0
UP_MAX = 0.5
PAIRS = 16
ROWS = 112
TILE = 128
RANKS = 8
FF = 2048


def code_of(most, bound):
    root = jnp.sqrt(jnp.sqrt(most * (1.0 / bound)))
    return jnp.clip(jnp.ceil(root * TOP), 1.0, TOP)


def step_of(code, bound):
    part = code * (1.0 / TOP)
    part = part * part
    return part * part * (bound / TOP)


def coded(values, code, bound):
    return jnp.clip(jnp.round(values / step_of(code, bound)), -TOP, TOP)


def to16(values):
    return values.astype(jnp.int32).astype(jnp.int16)


def spread_kernel(order_ref, up_ref, out_ref):
    for p in range(PAIRS):
        rows = jnp.concatenate([up_ref[order_ref[2 * p]], up_ref[order_ref[2 * p + 1]]] * 2, axis=0)
        for y in range(0, 32, 8):
            out_ref[p, y : y + 8, :] = rows


def spread(order, up):
    return pl.pallas_call(
        spread_kernel,
        in_specs=[pl.BlockSpec(memory_space=pltpu.SMEM), pl.BlockSpec(memory_space=pltpu.VMEM)],
        out_specs=pl.BlockSpec(memory_space=pltpu.VMEM),
        out_shape=jax.ShapeDtypeStruct((PAIRS, 32, TILE), jnp.float32),
        compiler_params=pltpu.CompilerParams(vmem_limit_bytes=4 * 2**20),
        cost_estimate=pl.CostEstimate(flops=0, bytes_accessed=300_000, transcendentals=0),
    )(order, up)


def code_kernel(up_ref, out_ref):
    most = jnp.zeros((32, TILE), jnp.float32)
    for r in range(PAIRS):
        most = jnp.maximum(most, jnp.abs(up_ref[r]))
    code = code_of(jnp.broadcast_to(jnp.max(most, axis=1, keepdims=True), (32, TILE)), UP_MAX)
    inverse = 1.0 / step_of(code, UP_MAX)
    for r in range(PAIRS):
        out_ref[:, r * TILE : (r + 1) * TILE] = to16(jnp.clip(jnp.round(up_ref[r] * inverse), -TOP, TOP))
    out_ref[:, FF : FF + TILE] = to16(code)


def code_up(up):
    return pl.pallas_call(
        code_kernel,
        in_specs=[pl.BlockSpec(memory_space=pltpu.VMEM)],
        out_specs=pl.BlockSpec(memory_space=pltpu.VMEM),
        out_shape=jax.ShapeDtypeStruct((32, FF + TILE), jnp.int16),
        compiler_params=pltpu.CompilerParams(vmem_limit_bytes=4 * 2**20),
        cost_estimate=pl.CostEstimate(flops=500_000, bytes_accessed=400_000, transcendentals=0),
    )(up)


def pack_kernel(per, order_ref, base_ref, down_ref, out_ref):
    first = pl.program_id(0) * per
    row8 = lax.broadcasted_iota(jnp.int32, (8, TILE), 0)
    lane = lax.broadcasted_iota(jnp.int32, (8, TILE), 1)
    for p in range(per):
        downs, base_codes = [], []
        for e in range(2):
            expert = order_ref[(first + p) * 2 + e]
            tile = base_ref[expert]
            code = code_of(jnp.max(jnp.abs(tile), axis=0, keepdims=True), BASE_MAX)
            inverse = 1.0 / step_of(code, BASE_MAX)
            out_ref[p, e, 0:ROWS, :] = to16(jnp.clip(jnp.round(tile * inverse), -TOP, TOP))
            base_codes.append(code)
            factor = down_ref[expert]
            most = jnp.max(jnp.abs(factor), axis=1, keepdims=True)
            code = code_of(jnp.broadcast_to(most, (RANKS, TILE)), DOWN_MAX)
            wide = jnp.concatenate([factor, jnp.zeros((RANKS, TILE - ROWS), jnp.float32)], axis=1)
            downs.append(jnp.where(lane < ROWS, coded(wide, code, DOWN_MAX), code))
        low = (row8 & 2) == 0
        own = jnp.where(low, downs[0], pltpu.roll(downs[1], 2, 0))
        other = jnp.where(low, pltpu.roll(downs[0], 6, 0), downs[1])
        out_ref[p, 0, ROWS:TILE, :] = to16(jnp.concatenate([own, other], axis=0))
        head = jnp.where(row8 == 0, base_codes[0], jnp.where(row8 == 1, base_codes[1], 0.0))
        out_ref[p, 1, ROWS:TILE, :] = to16(jnp.concatenate([head, jnp.zeros_like(head)], axis=0))


def pack(order, base, down):
    per = 4
    return pl.pallas_call(
        functools.partial(pack_kernel, per),
        grid_spec=pltpu.PrefetchScalarGridSpec(
            num_scalar_prefetch=1,
            grid=(PAIRS // per,),
            in_specs=[
                pl.BlockSpec(base.shape, lambda i, o: (0, 0, 0)),
                pl.BlockSpec(down.shape, lambda i, o: (0, 0, 0)),
            ],
            out_specs=pl.BlockSpec((per, 2, TILE, TILE), lambda i, o: (i, 0, 0, 0)),
        ),
        out_shape=jax.ShapeDtypeStruct((PAIRS, 2, TILE, TILE), jnp.int16),
        compiler_params=pltpu.CompilerParams(vmem_limit_bytes=24 * 2**20),
        cost_estimate=pl.CostEstimate(flops=4_000_000, bytes_accessed=3_000_000, transcendentals=0),
    )(order, base, down)


def sorted_rows(rows, xh):
    i = lax.broadcasted_iota(jnp.int32, (TILE, TILE), 0)
    j = lax.broadcasted_iota(jnp.int32, (TILE, TILE), 1)
    source = (((i >> 2) & 7) << 4) | (((i >> 5) ^ xh) << 2) | (i & 3)
    pick = jnp.where(j == source, 1.0, 0.0).astype(jnp.bfloat16)
    high = rows.astype(jnp.bfloat16)
    low = (rows - high.astype(jnp.float32)).astype(jnp.bfloat16)
    dot = functools.partial(jnp.dot, preferred_element_type=jnp.float32)
    return dot(pick, high) + dot(pick, low)


def merge_kernel(per, order_ref, flag_ref, place_ref, tile_ref, down_ref, own_ref, other_ref, own_code, other_code, out_ref, left_hi, left_lo):
    row, xh, core = place_ref[0], place_ref[1], place_ref[2]

    @pl.when(pl.program_id(0) == 0)
    def _():
        flags = [flag_ref[order_ref[2 * row + e]].astype(jnp.float32) for e in range(2)]
        rows = down_ref[:, 0, :, :].astype(jnp.float32)
        halves = [rows[:, 0:8, :].reshape(TILE, TILE), rows[:, 8:16, :].reshape(TILE, TILE)]
        mine = jnp.where(core == 0, halves[0], halves[1])
        theirs = jnp.where(core == 0, halves[1], halves[0])
        expert = (lax.broadcasted_iota(jnp.int32, (TILE, TILE), 0) >> 1) & 1
        for h, (factor, code_ref) in enumerate(((mine, own_code), (theirs, other_code))):
            factor = sorted_rows(factor, xh)
            scale = step_of(factor[:, ROWS : ROWS + 1], DOWN_MAX) * step_of(code_ref[...].astype(jnp.float32), UP_MAX)
            factor = factor * scale
            for e in range(2):
                part = jnp.where(expert == e, factor * flags[e], 0.0).T[0:ROWS, :]
                high = part.astype(jnp.bfloat16)
                left_hi[e * ROWS : (e + 1) * ROWS, h * TILE : (h + 1) * TILE] = high
                left_lo[e * ROWS : (e + 1) * ROWS, h * TILE : (h + 1) * TILE] = (part - high.astype(jnp.float32)).astype(jnp.bfloat16)

    right = jnp.concatenate([own_ref[...], other_ref[...]], axis=0).astype(jnp.float32)
    high = right.astype(jnp.bfloat16)
    low = (right - high.astype(jnp.float32)).astype(jnp.bfloat16)
    dot = functools.partial(jnp.dot, preferred_element_type=jnp.float32)
    delta = dot(left_hi[...], high) + (dot(left_lo[...], high) + dot(left_hi[...], low))
    for s in range(per):
        codes = tile_ref[s, 1, ROWS:TILE, :].astype(jnp.float32)
        for e in range(2):
            base = tile_ref[s, e, 0:ROWS, :].astype(jnp.float32) * step_of(codes[e : e + 1, :], BASE_MAX)
            total = base + delta[e * ROWS : (e + 1) * ROWS, s * TILE : (s + 1) * TILE]
            out_ref[e, :, s * TILE : (s + 1) * TILE] = total.astype(jnp.bfloat16)


def merge(order, flags, place, tiles, own, other):
    per = 4
    wide = per * TILE
    last = FF // TILE
    half = pl.BlockSpec((TILE, wide), lambda i, *_: (0, i))
    code = pl.BlockSpec((TILE, TILE), lambda i, *_: (0, last))
    return pl.pallas_call(
        functools.partial(merge_kernel, per),
        grid_spec=pltpu.PrefetchScalarGridSpec(
            num_scalar_prefetch=3,
            grid=(PAIRS // per,),
            in_specs=[
                pl.BlockSpec((per, 2, TILE, TILE), lambda i, *_: (i, 0, 0, 0)),
                pl.BlockSpec((PAIRS, 1, 16, TILE), lambda i, *_: (0, 0, ROWS // 16, 0)),
                half,
                half,
                code,
                code,
            ],
            out_specs=pl.BlockSpec((2, ROWS, wide), lambda i, *_: (0, 0, i)),
            scratch_shapes=[pltpu.VMEM((2 * ROWS, 2 * TILE), jnp.bfloat16)] * 2,
        ),
        out_shape=jax.ShapeDtypeStruct((2, ROWS, FF), jnp.bfloat16),
        compiler_params=pltpu.CompilerParams(vmem_limit_bytes=24 * 2**20),
        cost_estimate=pl.CostEstimate(flops=700_000_000, bytes_accessed=4_000_000, transcendentals=0),
    )(order, flags, place, tiles, tiles, own, other, own, other)


def body(base_weights, factor_down, factor_up, presence, serving_order):
    place = jnp.stack([lax.axis_index("row"), lax.axis_index("xh"), lax.axis_index("core")]).astype(jnp.int32)
    ups = spread(serving_order, factor_up).reshape(128, 4, TILE)
    ups = lax.all_to_all(ups, ("row", "y"), split_axis=0, concat_axis=0, tiled=True)
    sent = pack(serving_order, base_weights, jnp.swapaxes(factor_down, 1, 2))
    tiles = lax.all_to_all(sent, "row", split_axis=0, concat_axis=0, tiled=True)

    own = code_up(ups.reshape(PAIRS, 32, TILE))
    for apart in (1, 2):
        own = jnp.concatenate([own, lax.ppermute(own, "xh", [(i, i ^ apart) for i in range(4)])], axis=0)
    other = lax.ppermute(own, "core", [(0, 1), (1, 0)])
    return merge(serving_order, presence.reshape(-1), place, tiles, own, other)


def solution(mesh):
    fine = Mesh(mesh.devices.reshape(16, 8, 4, 2), ("row", "y", "xh", "core"))
    col = ("y", "xh", "core")
    return jax.shard_map(
        body,
        mesh=fine,
        in_specs=(P(None, col, "row"), P(None, col, "row"), P(None, col, "row"), P(), P()),
        out_specs=P("row", col, None),
        check_vma=False,
    )
```

```python
import functools

import jax
import jax.numpy as jnp
from jax import lax
from jax.experimental import pallas as pl
from jax.experimental.pallas import tpu as pltpu
from jax.sharding import Mesh, PartitionSpec as P

TOP = 32767.0
BASE_MAX = 6.0
DOWN_MAX = 6.0
UP_MAX = 0.5
PAIRS = 16
ROWS = 112
TILE = 128
RANKS = 8
FF = 2048


def code_of(most, bound):
    root = jnp.sqrt(jnp.sqrt(most * (1.0 / bound)))
    return jnp.clip(jnp.ceil(root * TOP), 1.0, TOP)


def step_of(code, bound):
    part = code * (1.0 / TOP)
    part = part * part
    return part * part * (bound / TOP)


def coded(values, code, bound):
    return jnp.clip(jnp.round(values / step_of(code, bound)), -TOP, TOP)


def to16(values):
    return values.astype(jnp.int32).astype(jnp.int16)


def spread_kernel(order_ref, up_ref, out_ref):
    for p in range(PAIRS):
        rows = jnp.concatenate([up_ref[order_ref[2 * p]], up_ref[order_ref[2 * p + 1]]] * 2, axis=0)
        root = jnp.minimum(jnp.round(jnp.sqrt(jnp.sqrt(jnp.abs(rows) * (1.0 / UP_MAX))) * TOP), TOP)
        root = jnp.where(rows < 0.0, -root, root)
        out_ref[p] = to16(jnp.concatenate([root] * 4, axis=0))


def spread(order, up):
    return pl.pallas_call(
        spread_kernel,
        in_specs=[pl.BlockSpec(memory_space=pltpu.SMEM), pl.BlockSpec(memory_space=pltpu.VMEM)],
        out_specs=pl.BlockSpec(memory_space=pltpu.VMEM),
        out_shape=jax.ShapeDtypeStruct((PAIRS, 32, TILE), jnp.int16),
        compiler_params=pltpu.CompilerParams(vmem_limit_bytes=4 * 2**20),
        cost_estimate=pl.CostEstimate(flops=0, bytes_accessed=300_000, transcendentals=0),
    )(order, up)


def code_kernel(up_ref, out_ref):
    most = jnp.zeros((32, TILE), jnp.float32)
    for r in range(PAIRS):
        most = jnp.maximum(most, jnp.abs(up_ref[r].astype(jnp.float32)))
    code = jnp.maximum(jnp.broadcast_to(jnp.max(most, axis=1, keepdims=True), (32, TILE)), 1.0)
    inverse = 1.0 / code
    for r in range(PAIRS):
        part = up_ref[r].astype(jnp.float32) * inverse
        part = part * part * part * jnp.abs(part)
        out_ref[:, r * TILE : (r + 1) * TILE] = to16(jnp.clip(jnp.round(part * TOP), -TOP, TOP))
    out_ref[:, FF : FF + TILE] = to16(code)


def code_up(up):
    return pl.pallas_call(
        code_kernel,
        in_specs=[pl.BlockSpec(memory_space=pltpu.VMEM)],
        out_specs=pl.BlockSpec(memory_space=pltpu.VMEM),
        out_shape=jax.ShapeDtypeStruct((32, FF + TILE), jnp.int16),
        compiler_params=pltpu.CompilerParams(vmem_limit_bytes=4 * 2**20),
        cost_estimate=pl.CostEstimate(flops=500_000, bytes_accessed=400_000, transcendentals=0),
    )(up)


def pack_kernel(per, order_ref, base_ref, down_ref, out_ref):
    first = pl.program_id(0) * per
    row8 = lax.broadcasted_iota(jnp.int32, (8, TILE), 0)
    lane = lax.broadcasted_iota(jnp.int32, (8, TILE), 1)
    for p in range(per):
        downs, base_codes = [], []
        for e in range(2):
            expert = order_ref[(first + p) * 2 + e]
            tile = base_ref[expert]
            code = code_of(jnp.max(jnp.abs(tile), axis=0, keepdims=True), BASE_MAX)
            inverse = 1.0 / step_of(code, BASE_MAX)
            out_ref[p, e, 0:ROWS, :] = to16(jnp.clip(jnp.round(tile * inverse), -TOP, TOP))
            base_codes.append(code)
            factor = down_ref[expert]
            most = jnp.max(jnp.abs(factor), axis=1, keepdims=True)
            code = code_of(jnp.broadcast_to(most, (RANKS, TILE)), DOWN_MAX)
            wide = jnp.concatenate([factor, jnp.zeros((RANKS, TILE - ROWS), jnp.float32)], axis=1)
            downs.append(jnp.where(lane < ROWS, coded(wide, code, DOWN_MAX), code))
        low = (row8 & 2) == 0
        own = jnp.where(low, downs[0], pltpu.roll(downs[1], 2, 0))
        other = jnp.where(low, pltpu.roll(downs[0], 6, 0), downs[1])
        out_ref[p, 0, ROWS:TILE, :] = to16(jnp.concatenate([own, other], axis=0))
        head = jnp.where(row8 == 0, base_codes[0], jnp.where(row8 == 1, base_codes[1], 0.0))
        out_ref[p, 1, ROWS:TILE, :] = to16(jnp.concatenate([head, jnp.zeros_like(head)], axis=0))


def pack(order, base, down):
    per = 4
    return pl.pallas_call(
        functools.partial(pack_kernel, per),
        grid_spec=pltpu.PrefetchScalarGridSpec(
            num_scalar_prefetch=1,
            grid=(PAIRS // per,),
            in_specs=[
                pl.BlockSpec(base.shape, lambda i, o: (0, 0, 0)),
                pl.BlockSpec(down.shape, lambda i, o: (0, 0, 0)),
            ],
            out_specs=pl.BlockSpec((per, 2, TILE, TILE), lambda i, o: (i, 0, 0, 0)),
        ),
        out_shape=jax.ShapeDtypeStruct((PAIRS, 2, TILE, TILE), jnp.int16),
        compiler_params=pltpu.CompilerParams(vmem_limit_bytes=24 * 2**20),
        cost_estimate=pl.CostEstimate(flops=4_000_000, bytes_accessed=3_000_000, transcendentals=0),
    )(order, base, down)


def sorted_rows(rows, yb):
    i = lax.broadcasted_iota(jnp.int32, (TILE, TILE), 0)
    j = lax.broadcasted_iota(jnp.int32, (TILE, TILE), 1)
    source = (((i >> 4) & 1) << 6) | (((i >> 5) ^ yb) << 4) | (i & 15)
    pick = jnp.where(j == source, 1.0, 0.0).astype(jnp.bfloat16)
    high = rows.astype(jnp.bfloat16)
    low = (rows - high.astype(jnp.float32)).astype(jnp.bfloat16)
    dot = functools.partial(jnp.dot, preferred_element_type=jnp.float32)
    return dot(pick, high) + dot(pick, low)


def merge_kernel(per, order_ref, flag_ref, place_ref, tile_ref, down_ref, own_ref, other_ref, own_code, other_code, out_ref, left_hi, left_lo):
    row, yb, core = place_ref[0], place_ref[1], place_ref[2]

    @pl.when(pl.program_id(0) == 0)
    def _():
        flags = [flag_ref[order_ref[2 * row + e]].astype(jnp.float32) for e in range(2)]
        rows = down_ref[:, 0, :, :].astype(jnp.float32)
        halves = [rows[:, 0:8, :].reshape(TILE, TILE), rows[:, 8:16, :].reshape(TILE, TILE)]
        mine = jnp.where(core == 0, halves[0], halves[1])
        theirs = jnp.where(core == 0, halves[1], halves[0])
        expert = (lax.broadcasted_iota(jnp.int32, (TILE, TILE), 0) >> 1) & 1
        for h, (factor, code_ref) in enumerate(((mine, own_code), (theirs, other_code))):
            factor = sorted_rows(factor, yb)
            scale = step_of(factor[:, ROWS : ROWS + 1], DOWN_MAX) * step_of(code_ref[...].astype(jnp.float32), UP_MAX)
            factor = factor * scale
            for e in range(2):
                part = jnp.where(expert == e, factor * flags[e], 0.0).T[0:ROWS, :]
                high = part.astype(jnp.bfloat16)
                left_hi[e * ROWS : (e + 1) * ROWS, h * TILE : (h + 1) * TILE] = high
                left_lo[e * ROWS : (e + 1) * ROWS, h * TILE : (h + 1) * TILE] = (part - high.astype(jnp.float32)).astype(jnp.bfloat16)

    right = jnp.concatenate([own_ref[...], other_ref[...]], axis=0).astype(jnp.float32)
    high = right.astype(jnp.bfloat16)
    low = (right - high.astype(jnp.float32)).astype(jnp.bfloat16)
    dot = functools.partial(jnp.dot, preferred_element_type=jnp.float32)
    delta = dot(left_hi[...], high) + (dot(left_lo[...], high) + dot(left_hi[...], low))
    for s in range(per):
        codes = tile_ref[s, 1, ROWS:TILE, :].astype(jnp.float32)
        for e in range(2):
            base = tile_ref[s, e, 0:ROWS, :].astype(jnp.float32) * step_of(codes[e : e + 1, :], BASE_MAX)
            total = base + delta[e * ROWS : (e + 1) * ROWS, s * TILE : (s + 1) * TILE]
            out_ref[e, :, s * TILE : (s + 1) * TILE] = total.astype(jnp.bfloat16)


def merge(order, flags, place, tiles, own, other):
    per = 4
    wide = per * TILE
    last = FF // TILE
    half = pl.BlockSpec((TILE, wide), lambda i, *_: (0, i))
    code = pl.BlockSpec((TILE, TILE), lambda i, *_: (0, last))
    return pl.pallas_call(
        functools.partial(merge_kernel, per),
        grid_spec=pltpu.PrefetchScalarGridSpec(
            num_scalar_prefetch=3,
            grid=(PAIRS // per,),
            in_specs=[
                pl.BlockSpec((per, 2, TILE, TILE), lambda i, *_: (i, 0, 0, 0)),
                pl.BlockSpec((PAIRS, 1, 16, TILE), lambda i, *_: (0, 0, ROWS // 16, 0)),
                half,
                half,
                code,
                code,
            ],
            out_specs=pl.BlockSpec((2, ROWS, wide), lambda i, *_: (0, 0, i)),
            scratch_shapes=[pltpu.VMEM((2 * ROWS, 2 * TILE), jnp.bfloat16)] * 2,
        ),
        out_shape=jax.ShapeDtypeStruct((2, ROWS, FF), jnp.bfloat16),
        compiler_params=pltpu.CompilerParams(vmem_limit_bytes=24 * 2**20),
        cost_estimate=pl.CostEstimate(flops=700_000_000, bytes_accessed=4_000_000, transcendentals=0),
    )(order, flags, place, tiles, tiles, own, other, own, other)


def body(base_weights, factor_down, factor_up, presence, serving_order):
    place = jnp.stack([lax.axis_index("row"), lax.axis_index("yb"), lax.axis_index("core")]).astype(jnp.int32)
    ups = spread(serving_order, factor_up).reshape(128, 4, TILE)
    ups = lax.all_to_all(ups, ("row", "ya", "xh"), split_axis=0, concat_axis=0, tiled=True)
    sent = pack(serving_order, base_weights, jnp.swapaxes(factor_down, 1, 2))
    tiles = lax.all_to_all(sent, "row", split_axis=0, concat_axis=0, tiled=True)

    own = code_up(ups.reshape(PAIRS, 32, TILE))
    own = jnp.concatenate([own] + [lax.ppermute(own, "yb", [(i, i ^ apart) for i in range(4)]) for apart in (1, 2, 3)], axis=0)
    other = lax.ppermute(own, "core", [(0, 1), (1, 0)])
    return merge(serving_order, presence.reshape(-1), place, tiles, own, other)


def solution(mesh):
    fine = Mesh(mesh.devices.reshape(16, 2, 4, 4, 2), ("row", "ya", "yb", "xh", "core"))
    col = ("ya", "yb", "xh", "core")
    return jax.shard_map(
        body,
        mesh=fine,
        in_specs=(P(None, col, "row"), P(None, col, "row"), P(None, col, "row"), P(), P()),
        out_specs=P("row", col, None),
        check_vma=False,
    )
```

```python
import functools

import jax
import jax.numpy as jnp
from jax import lax
from jax.experimental import pallas as pl
from jax.experimental.pallas import tpu as pltpu
from jax.sharding import Mesh, PartitionSpec as P

TOP = 32767.0
BASE_MAX = 6.0
DOWN_MAX = 6.0
UP_MAX = 0.5
PAIRS = 16
ROWS = 112
TILE = 128
RANKS = 8
FF = 2048
PACKED = 2 * ROWS + 16
CODE = ROWS
DOT = functools.partial(jnp.dot, preferred_element_type=jnp.float32)


def code_of(most, bound):
    root = jnp.sqrt(jnp.sqrt(most * (1.0 / bound)))
    return jnp.clip(jnp.ceil(root * TOP), 1.0, TOP)


def scale_of(code, bound):
    part = code * (1.0 / TOP)
    part = part * part
    return part * part * bound


def signed(root, values):
    root = jnp.minimum(jnp.round(root * TOP), TOP)
    return jnp.where(values < 0.0, -root, root)


def to16(values):
    return values.astype(jnp.int32).astype(jnp.int16)


def halves(values):
    high = values.astype(jnp.bfloat16)
    return high, (values - high.astype(jnp.float32)).astype(jnp.bfloat16)


def order_up_kernel(order_ref, up_ref, out_ref):
    for p in range(0, PAIRS, 4):
        rows = jnp.concatenate([up_ref[order_ref[2 * p + i]] for i in range(8)], axis=0)
        root = jnp.sqrt(jnp.sqrt(jnp.abs(rows) * (1.0 / UP_MAX)))
        out_ref[4 * p : 4 * p + 16, :] = to16(signed(root, rows))


def order_up(order, up):
    return pl.pallas_call(
        order_up_kernel,
        in_specs=[pl.BlockSpec(memory_space=pltpu.SMEM), pl.BlockSpec(memory_space=pltpu.VMEM)],
        out_specs=pl.BlockSpec(memory_space=pltpu.VMEM),
        out_shape=jax.ShapeDtypeStruct((PAIRS * 4, TILE), jnp.int16),
        compiler_params=pltpu.CompilerParams(vmem_limit_bytes=60 * 2**20),
        cost_estimate=pl.CostEstimate(flops=0, bytes_accessed=300_000, transcendentals=0),
    )(order, up)


def pack_kernel(per, order_ref, base_ref, down_ref, out_ref):
    first = pl.program_id(0) * per
    row8 = lax.broadcasted_iota(jnp.int32, (8, TILE), 0)
    lane = lax.broadcasted_iota(jnp.int32, (8, TILE), 1)
    for p in range(per):
        downs, base_codes = [], []
        for e in range(2):
            expert = order_ref[(first + p) * 2 + e]
            tile = base_ref[expert]
            size = jnp.abs(tile)
            most = jnp.max(jnp.max(size, axis=0, keepdims=True), axis=1, keepdims=True)
            code = code_of(jnp.broadcast_to(most, (1, TILE)), BASE_MAX)
            root = jnp.sqrt(size * (1.0 / scale_of(code, BASE_MAX)))
            out_ref[p, e * ROWS : (e + 1) * ROWS, :] = to16(signed(root, tile))
            base_codes.append(code)
            factor = down_ref[expert]
            most = jnp.max(jnp.abs(factor), axis=1, keepdims=True)
            code = code_of(jnp.broadcast_to(most, (RANKS, TILE)), DOWN_MAX)
            wide = jnp.concatenate([factor, jnp.zeros((RANKS, TILE - ROWS), jnp.float32)], axis=1)
            root = jnp.sqrt(jnp.abs(wide) * (1.0 / scale_of(code, DOWN_MAX)))
            downs.append(jnp.where(lane < CODE, signed(root, wide), code))
        low = (row8 & 2) == 0
        own = jnp.where(low, downs[0], pltpu.roll(downs[1], 2, 0))
        other = jnp.where(low, pltpu.roll(downs[0], 6, 0), downs[1])
        rows = jnp.concatenate([own, other], axis=0)
        lanes = jnp.concatenate([lane, lane], axis=0)
        for e in range(2):
            rows = jnp.where(lanes == CODE + 1 + e, base_codes[e], rows)
        out_ref[p, 2 * ROWS : PACKED, :] = to16(rows)


def pack(order, base, down):
    per = 4
    return pl.pallas_call(
        functools.partial(pack_kernel, per),
        grid_spec=pltpu.PrefetchScalarGridSpec(
            num_scalar_prefetch=1,
            grid=(PAIRS // per,),
            in_specs=[
                pl.BlockSpec(base.shape, lambda i, o: (0, 0, 0)),
                pl.BlockSpec(down.shape, lambda i, o: (0, 0, 0)),
            ],
            out_specs=pl.BlockSpec((per, PACKED, TILE), lambda i, o: (i, 0, 0)),
        ),
        out_shape=jax.ShapeDtypeStruct((PAIRS, PACKED, TILE), jnp.int16),
        compiler_params=pltpu.CompilerParams(vmem_limit_bytes=60 * 2**20),
        cost_estimate=pl.CostEstimate(flops=4_000_000, bytes_accessed=3_000_000, transcendentals=0),
    )(order, base, down)


def sorted_rows(rows, yb):
    i = lax.broadcasted_iota(jnp.int32, (TILE, TILE), 0)
    j = lax.broadcasted_iota(jnp.int32, (TILE, TILE), 1)
    source = (((i >> 4) & 1) << 6) | (((i >> 5) ^ yb) << 4) | (i & 15)
    pick = jnp.where(j == source, 1.0, 0.0).astype(jnp.bfloat16)
    high, low = halves(rows)
    return DOT(pick, high) + DOT(pick, low)


def merge_kernel(per, order_ref, flag_ref, place_ref, tile_ref, down_ref, own_ref, other_ref, out_ref, left_hi, left_lo):
    row, yb, core = place_ref[0], place_ref[1], place_ref[2]

    @pl.when(pl.program_id(0) == 0)
    def _():
        flags = [flag_ref[order_ref[2 * row + e]].astype(jnp.float32) for e in range(2)]
        rows = down_ref[...].astype(jnp.float32)
        cores = [rows[:, 0:8, :].reshape(TILE, TILE), rows[:, 8:16, :].reshape(TILE, TILE)]
        mine = jnp.where(core == 0, cores[0], cores[1])
        theirs = jnp.where(core == 0, cores[1], cores[0])
        expert = (lax.broadcasted_iota(jnp.int32, (TILE, TILE), 0) >> 1) & 1
        for h, factor in enumerate((mine, theirs)):
            factor = sorted_rows(factor, yb)
            scale = scale_of(factor[:, CODE : CODE + 1], DOWN_MAX) * (UP_MAX / TOP**2)
            factor = factor * jnp.abs(factor) * scale
            for e in range(2):
                part = jnp.where(expert == e, factor * flags[e], 0.0).T[0:ROWS, :]
                at = (slice(e * ROWS, (e + 1) * ROWS), slice(h * TILE, (h + 1) * TILE))
                left_hi[at], left_lo[at] = halves(part)

    ups = jnp.concatenate([jnp.concatenate([own_ref[s], other_ref[s]], axis=0) for s in range(per)], axis=1)
    ups = ups.astype(jnp.float32) * (1.0 / TOP)
    square = ups * ups
    high, low = halves(square * (ups * jnp.abs(ups)))
    delta = DOT(left_hi[...], high) + (DOT(left_lo[...], high) + DOT(left_hi[...], low))
    for s in range(per):
        codes = tile_ref[s, 2 * ROWS : PACKED, :].astype(jnp.float32)
        for e in range(2):
            scale = scale_of(codes[0:1, CODE + 1 + e : CODE + 2 + e], BASE_MAX) * (1.0 / TOP**2)
            base = tile_ref[s, e * ROWS : (e + 1) * ROWS, :].astype(jnp.float32)
            total = base * jnp.abs(base) * scale + delta[e * ROWS : (e + 1) * ROWS, s * TILE : (s + 1) * TILE]
            out_ref[e, :, s * TILE : (s + 1) * TILE] = total.astype(jnp.bfloat16)


def merge(order, flags, place, tiles, own, other):
    per = 4
    half = pl.BlockSpec((per, TILE, TILE), lambda i, *_: (i, 0, 0))
    return pl.pallas_call(
        functools.partial(merge_kernel, per),
        grid_spec=pltpu.PrefetchScalarGridSpec(
            num_scalar_prefetch=3,
            grid=(PAIRS // per,),
            in_specs=[
                pl.BlockSpec((per, PACKED, TILE), lambda i, *_: (i, 0, 0)),
                pl.BlockSpec((PAIRS, 16, TILE), lambda i, *_: (0, 2 * ROWS // 16, 0)),
                half,
                half,
            ],
            out_specs=pl.BlockSpec((2, ROWS, per * TILE), lambda i, *_: (0, 0, i)),
            scratch_shapes=[pltpu.VMEM((2 * ROWS, 2 * TILE), jnp.bfloat16)] * 2,
        ),
        out_shape=jax.ShapeDtypeStruct((2, ROWS, FF), jnp.bfloat16),
        compiler_params=pltpu.CompilerParams(vmem_limit_bytes=24 * 2**20),
        cost_estimate=pl.CostEstimate(flops=700_000_000, bytes_accessed=4_000_000, transcendentals=0),
    )(order, flags, place, tiles, tiles, own, other)


def body(base_weights, factor_down, factor_up, presence, serving_order):
    place = jnp.stack([lax.axis_index("row"), lax.axis_index("yb"), lax.axis_index("core")]).astype(jnp.int32)
    exchange = functools.partial(lax.all_to_all, split_axis=0, concat_axis=0, tiled=True)
    ups = exchange(order_up(serving_order, factor_up).reshape(PAIRS, 4, TILE), "row")
    ups = exchange(jnp.broadcast_to(ups[None], (8, PAIRS, 4, TILE)), ("ya", "xh"))
    sent = pack(serving_order, base_weights, jnp.swapaxes(factor_down, 1, 2))
    tiles = exchange(sent, "row")

    own = jnp.swapaxes(ups, 0, 1).reshape(PAIRS, 32, TILE)
    own = jnp.concatenate([own] + [lax.ppermute(own, "yb", [(i, i ^ apart) for i in range(4)]) for apart in (1, 2, 3)], axis=1)
    other = lax.ppermute(own, "core", [(0, 1), (1, 0)])
    return merge(serving_order, presence.reshape(-1), place, tiles, own, other)


def solution(mesh):
    fine = Mesh(mesh.devices.reshape(16, 2, 4, 4, 2), ("row", "ya", "yb", "xh", "core"))
    col = ("ya", "yb", "xh", "core")
    return jax.shard_map(
        body,
        mesh=fine,
        in_specs=(P(None, col, "row"), P(None, col, "row"), P(None, col, "row"), P(), P()),
        out_specs=P("row", col, None),
        check_vma=False,
    )
```

```python
import functools

import jax
import jax.numpy as jnp
from jax import lax
from jax.experimental import pallas as pl
from jax.experimental.pallas import tpu as pltpu
from jax.sharding import Mesh, PartitionSpec as P

TOP = 32767.0
BASE_MAX = 6.0
DOWN_MAX = 6.0
UP_MAX = 0.5
PAIRS = 16
ROWS = 112
TILE = 128
RANKS = 8
FF = 2048
PACKED = 2 * ROWS + 16
CODE = ROWS
DOT = functools.partial(jnp.dot, preferred_element_type=jnp.float32)


def code_of(most, bound):
    root = jnp.sqrt(jnp.sqrt(most * (1.0 / bound)))
    return jnp.clip(jnp.ceil(root * TOP), 1.0, TOP)


def scale_of(code, bound):
    part = code * (1.0 / TOP)
    part = part * part
    return part * part * bound


def signed(root, values):
    root = jnp.minimum(jnp.round(root * TOP), TOP)
    return jnp.where(values < 0.0, -root, root)


def to16(values):
    return values.astype(jnp.int32).astype(jnp.int16)


def halves(values):
    high = values.astype(jnp.bfloat16)
    return high, (values - high.astype(jnp.float32)).astype(jnp.bfloat16)


def order_up_kernel(order_ref, up_ref, out_ref):
    for p in range(PAIRS):
        rows = jnp.concatenate([up_ref[order_ref[2 * p]], up_ref[order_ref[2 * p + 1]]] * 2, axis=0)
        root = jnp.sqrt(jnp.sqrt(jnp.abs(rows) * (1.0 / UP_MAX)))
        out_ref[p] = to16(jnp.concatenate([signed(root, rows)] * 4, axis=0))


def order_up(order, up):
    return pl.pallas_call(
        order_up_kernel,
        in_specs=[pl.BlockSpec(memory_space=pltpu.SMEM), pl.BlockSpec(memory_space=pltpu.VMEM)],
        out_specs=pl.BlockSpec(memory_space=pltpu.VMEM),
        out_shape=jax.ShapeDtypeStruct((PAIRS, 32, TILE), jnp.int16),
        compiler_params=pltpu.CompilerParams(vmem_limit_bytes=60 * 2**20),
        cost_estimate=pl.CostEstimate(flops=0, bytes_accessed=300_000, transcendentals=0),
    )(order, up)


def pack_kernel(per, order_ref, base_ref, down_ref, out_ref):
    first = pl.program_id(0) * per
    row8 = lax.broadcasted_iota(jnp.int32, (8, TILE), 0)
    lane = lax.broadcasted_iota(jnp.int32, (8, TILE), 1)
    for p in range(per):
        downs, base_codes = [], []
        for e in range(2):
            expert = order_ref[(first + p) * 2 + e]
            tile = base_ref[expert]
            size = jnp.abs(tile)
            most = jnp.max(jnp.max(size, axis=0, keepdims=True), axis=1, keepdims=True)
            code = code_of(jnp.broadcast_to(most, (1, TILE)), BASE_MAX)
            root = jnp.sqrt(size * (1.0 / scale_of(code, BASE_MAX)))
            out_ref[p, e * ROWS : (e + 1) * ROWS, :] = to16(signed(root, tile))
            base_codes.append(code)
            factor = down_ref[expert]
            most = jnp.max(jnp.abs(factor), axis=1, keepdims=True)
            code = code_of(jnp.broadcast_to(most, (RANKS, TILE)), DOWN_MAX)
            wide = jnp.concatenate([factor, jnp.zeros((RANKS, TILE - ROWS), jnp.float32)], axis=1)
            root = jnp.sqrt(jnp.abs(wide) * (1.0 / scale_of(code, DOWN_MAX)))
            downs.append(jnp.where(lane < CODE, signed(root, wide), code))
        low = (row8 & 2) == 0
        own = jnp.where(low, downs[0], pltpu.roll(downs[1], 2, 0))
        other = jnp.where(low, pltpu.roll(downs[0], 6, 0), downs[1])
        rows = jnp.concatenate([own, other], axis=0)
        lanes = jnp.concatenate([lane, lane], axis=0)
        for e in range(2):
            rows = jnp.where(lanes == CODE + 1 + e, base_codes[e], rows)
        out_ref[p, 2 * ROWS : PACKED, :] = to16(rows)


def pack(order, base, down):
    per = 4
    return pl.pallas_call(
        functools.partial(pack_kernel, per),
        grid_spec=pltpu.PrefetchScalarGridSpec(
            num_scalar_prefetch=1,
            grid=(PAIRS // per,),
            in_specs=[
                pl.BlockSpec(base.shape, lambda i, o: (0, 0, 0)),
                pl.BlockSpec(down.shape, lambda i, o: (0, 0, 0)),
            ],
            out_specs=pl.BlockSpec((per, PACKED, TILE), lambda i, o: (i, 0, 0)),
        ),
        out_shape=jax.ShapeDtypeStruct((PAIRS, PACKED, TILE), jnp.int16),
        compiler_params=pltpu.CompilerParams(vmem_limit_bytes=60 * 2**20),
        cost_estimate=pl.CostEstimate(flops=4_000_000, bytes_accessed=3_000_000, transcendentals=0),
    )(order, base, down)


def sorted_rows(rows, yb):
    i = lax.broadcasted_iota(jnp.int32, (TILE, TILE), 0)
    j = lax.broadcasted_iota(jnp.int32, (TILE, TILE), 1)
    source = (((i >> 4) & 1) << 6) | (((i >> 5) ^ yb) << 4) | (i & 15)
    pick = jnp.where(j == source, 1.0, 0.0).astype(jnp.bfloat16)
    high, low = halves(rows)
    return DOT(pick, high) + DOT(pick, low)


def merge_kernel(per, order_ref, flag_ref, place_ref, tile_ref, down_ref, own_ref, other_ref, out_ref, left_hi, left_lo):
    row, yb, core = place_ref[0], place_ref[1], place_ref[2]

    @pl.when(pl.program_id(0) == 0)
    def _():
        flags = [flag_ref[order_ref[2 * row + e]].astype(jnp.float32) for e in range(2)]
        rows = down_ref[...].astype(jnp.float32)
        cores = [rows[:, 0:8, :].reshape(TILE, TILE), rows[:, 8:16, :].reshape(TILE, TILE)]
        mine = jnp.where(core == 0, cores[0], cores[1])
        theirs = jnp.where(core == 0, cores[1], cores[0])
        expert = (lax.broadcasted_iota(jnp.int32, (TILE, TILE), 0) >> 1) & 1
        for h, factor in enumerate((mine, theirs)):
            factor = sorted_rows(factor, yb)
            scale = scale_of(factor[:, CODE : CODE + 1], DOWN_MAX) * (UP_MAX / TOP**2)
            factor = factor * jnp.abs(factor) * scale
            for e in range(2):
                part = jnp.where(expert == e, factor * flags[e], 0.0).T[0:ROWS, :]
                at = (slice(e * ROWS, (e + 1) * ROWS), slice(h * TILE, (h + 1) * TILE))
                left_hi[at], left_lo[at] = halves(part)

    ups = jnp.concatenate([jnp.concatenate([own_ref[s], other_ref[s]], axis=0) for s in range(per)], axis=1)
    ups = ups.astype(jnp.float32) * (1.0 / TOP)
    square = ups * ups
    high, low = halves(square * (ups * jnp.abs(ups)))
    delta = DOT(left_hi[...], high) + (DOT(left_lo[...], high) + DOT(left_hi[...], low))
    for s in range(per):
        codes = tile_ref[s, 2 * ROWS : PACKED, :].astype(jnp.float32)
        for e in range(2):
            scale = scale_of(codes[0:1, CODE + 1 + e : CODE + 2 + e], BASE_MAX) * (1.0 / TOP**2)
            base = tile_ref[s, e * ROWS : (e + 1) * ROWS, :].astype(jnp.float32)
            total = base * jnp.abs(base) * scale + delta[e * ROWS : (e + 1) * ROWS, s * TILE : (s + 1) * TILE]
            out_ref[e, :, s * TILE : (s + 1) * TILE] = total.astype(jnp.bfloat16)


def merge(order, flags, place, tiles, own, other):
    per = 4
    half = pl.BlockSpec((per, TILE, TILE), lambda i, *_: (i, 0, 0))
    return pl.pallas_call(
        functools.partial(merge_kernel, per),
        grid_spec=pltpu.PrefetchScalarGridSpec(
            num_scalar_prefetch=3,
            grid=(PAIRS // per,),
            in_specs=[
                pl.BlockSpec((per, PACKED, TILE), lambda i, *_: (i, 0, 0)),
                pl.BlockSpec((PAIRS, 16, TILE), lambda i, *_: (0, 2 * ROWS // 16, 0)),
                half,
                half,
            ],
            out_specs=pl.BlockSpec((2, ROWS, per * TILE), lambda i, *_: (0, 0, i)),
            scratch_shapes=[pltpu.VMEM((2 * ROWS, 2 * TILE), jnp.bfloat16)] * 2,
        ),
        out_shape=jax.ShapeDtypeStruct((2, ROWS, FF), jnp.bfloat16),
        compiler_params=pltpu.CompilerParams(vmem_limit_bytes=24 * 2**20),
        cost_estimate=pl.CostEstimate(flops=700_000_000, bytes_accessed=4_000_000, transcendentals=0),
    )(order, flags, place, tiles, tiles, own, other)


def body(base_weights, factor_down, factor_up, presence, serving_order):
    place = jnp.stack([lax.axis_index("row"), lax.axis_index("yb"), lax.axis_index("core")]).astype(jnp.int32)
    exchange = functools.partial(lax.all_to_all, split_axis=0, concat_axis=0, tiled=True)
    ups = exchange(order_up(serving_order, factor_up).reshape(128, 4, TILE), ("row", "ya", "xh"))
    sent = pack(serving_order, base_weights, jnp.swapaxes(factor_down, 1, 2))
    tiles = exchange(sent, "row")

    own = ups.reshape(PAIRS, 32, TILE)
    own = jnp.concatenate([own] + [lax.ppermute(own, "yb", [(i, i ^ apart) for i in range(4)]) for apart in (1, 2, 3)], axis=1)
    other = lax.ppermute(own, "core", [(0, 1), (1, 0)])
    return merge(serving_order, presence.reshape(-1), place, tiles, own, other)


def solution(mesh):
    fine = Mesh(mesh.devices.reshape(16, 2, 4, 4, 2), ("row", "ya", "yb", "xh", "core"))
    col = ("ya", "yb", "xh", "core")
    return jax.shard_map(
        body,
        mesh=fine,
        in_specs=(P(None, col, "row"), P(None, col, "row"), P(None, col, "row"), P(), P()),
        out_specs=P("row", col, None),
        check_vma=False,
    )
```

```python
import functools

import jax
import jax.numpy as jnp
from jax import lax
from jax.experimental import pallas as pl
from jax.experimental.pallas import tpu as pltpu
from jax.sharding import Mesh, PartitionSpec as P

TOP = 32767.0
BASE_MAX = 6.0
DOWN_MAX = 6.0
UP_MAX = 0.5
PAIRS = 16
ROWS = 112
TILE = 128
RANKS = 8
FF = 2048
PACKED = 2 * ROWS + 16
CODE = ROWS
DOT = functools.partial(jnp.dot, preferred_element_type=jnp.float32)


def code_of(most, bound):
    root = jnp.sqrt(jnp.sqrt(most * (1.0 / bound)))
    return jnp.clip(jnp.ceil(root * TOP), 1.0, TOP)


def scale_of(code, bound):
    part = code * (1.0 / TOP)
    part = part * part
    return part * part * bound


def signed(root, values):
    root = jnp.minimum(jnp.round(root * TOP), TOP)
    return jnp.where(values < 0.0, -root, root)


def to16(values):
    return values.astype(jnp.int32).astype(jnp.int16)


def halves(values):
    high = values.astype(jnp.bfloat16)
    return high, (values - high.astype(jnp.float32)).astype(jnp.bfloat16)


def order_up_kernel(order_ref, up_ref, out_ref):
    for p in range(PAIRS):
        rows = jnp.concatenate([up_ref[order_ref[2 * p]], up_ref[order_ref[2 * p + 1]]] * 2, axis=0)
        root = jnp.sqrt(jnp.sqrt(jnp.abs(rows) * (1.0 / UP_MAX)))
        out_ref[p] = to16(jnp.concatenate([signed(root, rows)] * 2, axis=0))


def order_up(order, up):
    return pl.pallas_call(
        order_up_kernel,
        in_specs=[pl.BlockSpec(memory_space=pltpu.SMEM), pl.BlockSpec(memory_space=pltpu.VMEM)],
        out_specs=pl.BlockSpec(memory_space=pltpu.VMEM),
        out_shape=jax.ShapeDtypeStruct((PAIRS, 16, TILE), jnp.int16),
        compiler_params=pltpu.CompilerParams(vmem_limit_bytes=60 * 2**20),
        cost_estimate=pl.CostEstimate(flops=0, bytes_accessed=300_000, transcendentals=0),
    )(order, up)


def pack_kernel(per, order_ref, base_ref, down_ref, out_ref):
    first = pl.program_id(0) * per
    row8 = lax.broadcasted_iota(jnp.int32, (8, TILE), 0)
    lane = lax.broadcasted_iota(jnp.int32, (8, TILE), 1)
    for p in range(per):
        downs, base_codes = [], []
        for e in range(2):
            expert = order_ref[(first + p) * 2 + e]
            tile = base_ref[expert]
            size = jnp.abs(tile)
            most = jnp.max(jnp.max(size, axis=0, keepdims=True), axis=1, keepdims=True)
            code = code_of(jnp.broadcast_to(most, (1, TILE)), BASE_MAX)
            root = jnp.sqrt(size * (1.0 / scale_of(code, BASE_MAX)))
            out_ref[p, e * ROWS : (e + 1) * ROWS, :] = to16(signed(root, tile))
            base_codes.append(code)
            factor = down_ref[expert]
            most = jnp.max(jnp.abs(factor), axis=1, keepdims=True)
            code = code_of(jnp.broadcast_to(most, (RANKS, TILE)), DOWN_MAX)
            wide = jnp.concatenate([factor, jnp.zeros((RANKS, TILE - ROWS), jnp.float32)], axis=1)
            root = jnp.sqrt(jnp.abs(wide) * (1.0 / scale_of(code, DOWN_MAX)))
            downs.append(jnp.where(lane < CODE, signed(root, wide), code))
        low = (row8 & 2) == 0
        own = jnp.where(low, downs[0], pltpu.roll(downs[1], 2, 0))
        other = jnp.where(low, pltpu.roll(downs[0], 6, 0), downs[1])
        rows = jnp.concatenate([own, other], axis=0)
        lanes = jnp.concatenate([lane, lane], axis=0)
        for e in range(2):
            rows = jnp.where(lanes == CODE + 1 + e, base_codes[e], rows)
        out_ref[p, 2 * ROWS : PACKED, :] = to16(rows)


def pack(order, base, down):
    per = 4
    return pl.pallas_call(
        functools.partial(pack_kernel, per),
        grid_spec=pltpu.PrefetchScalarGridSpec(
            num_scalar_prefetch=1,
            grid=(PAIRS // per,),
            in_specs=[
                pl.BlockSpec(base.shape, lambda i, o: (0, 0, 0)),
                pl.BlockSpec(down.shape, lambda i, o: (0, 0, 0)),
            ],
            out_specs=pl.BlockSpec((per, PACKED, TILE), lambda i, o: (i, 0, 0)),
        ),
        out_shape=jax.ShapeDtypeStruct((PAIRS, PACKED, TILE), jnp.int16),
        compiler_params=pltpu.CompilerParams(vmem_limit_bytes=60 * 2**20),
        cost_estimate=pl.CostEstimate(flops=4_000_000, bytes_accessed=3_000_000, transcendentals=0),
    )(order, base, down)


def sorted_rows(rows, y, core):
    i = lax.broadcasted_iota(jnp.int32, (2 * TILE, 2 * TILE), 0)
    j = lax.broadcasted_iota(jnp.int32, (2 * TILE, 2 * TILE), 1)
    taker = jnp.where(i < 144, core, 1 - core)
    at = jnp.where(i < 32, i, jnp.where(i < 144, i - 32, i - 144))
    single = at >= 96
    apart = jnp.where(i < 32, 0, jnp.where(single, 4, (at >> 5) + 1 + 4 * taker))
    of = jnp.where(single, taker, taker ^ ((at >> 4) & 1))
    pick = jnp.where(j == ((of << 7) | ((y ^ apart) << 4) | (i & 15)), 1.0, 0.0).astype(jnp.bfloat16)
    high, low = halves(rows)
    return DOT(pick, high) + DOT(pick, low)


def merge_kernel(order_ref, flag_ref, place_ref, tile_ref, both_ref, mine_ref, other_ref, out_ref, left_hi, left_lo, done, sent):
    row, y, core = place_ref[0], place_ref[1], place_ref[2]
    rows = tile_ref[:, 2 * ROWS : PACKED, :].astype(jnp.float32)
    rows = jnp.concatenate([rows[:, 0:8, :].reshape(TILE, TILE), rows[:, 8:16, :].reshape(TILE, TILE)], axis=0)
    factor = sorted_rows(rows, y, core)
    scale = scale_of(factor[:, CODE : CODE + 1], DOWN_MAX) * (UP_MAX / TOP**2)
    factor = factor * jnp.abs(factor) * scale
    expert = (lax.broadcasted_iota(jnp.int32, (2 * TILE, TILE), 0) >> 1) & 1
    for e in range(2):
        flag = flag_ref[order_ref[2 * row + e]].astype(jnp.float32)
        part = jnp.where(expert == e, factor * flag, 0.0).T[0:ROWS, :]
        at = slice(e * ROWS, (e + 1) * ROWS)
        left_hi[at, :], left_lo[at, :] = halves(part)

    wide = 4
    for i in range(PAIRS // wide):
        spots = range(i * wide, (i + 1) * wide)
        ups = jnp.concatenate([jnp.concatenate([both_ref[s], mine_ref[s], other_ref[s]], axis=0) for s in spots], axis=1)
        ups = ups.astype(jnp.float32) * (1.0 / TOP)
        square = ups * ups
        high, low = halves(square * (ups * jnp.abs(ups)))
        delta = DOT(left_hi[...], high) + (DOT(left_lo[...], high) + DOT(left_hi[...], low))
        for at, s in enumerate(spots):
            codes = tile_ref[s, 2 * ROWS : PACKED, :].astype(jnp.float32)
            for e in range(2):
                scale = scale_of(codes[0:1, CODE + 1 + e : CODE + 2 + e], BASE_MAX) * (1.0 / TOP**2)
                base = tile_ref[s, e * ROWS : (e + 1) * ROWS, :].astype(jnp.float32)
                total = base * jnp.abs(base) * scale + delta[e * ROWS : (e + 1) * ROWS, at * TILE : (at + 1) * TILE]
                done[i, e, :, at * TILE : (at + 1) * TILE] = total.astype(jnp.bfloat16)
        pltpu.make_async_copy(done.at[i], out_ref.at[:, :, pl.ds(i * wide * TILE, wide * TILE)], sent.at[i]).start()
    for i in range(PAIRS // wide):
        pltpu.make_async_copy(done.at[i], out_ref.at[:, :, pl.ds(i * wide * TILE, wide * TILE)], sent.at[i]).wait()


def merge(order, flags, place, tiles, ups):
    wide = 4
    smem, vmem = pl.BlockSpec(memory_space=pltpu.SMEM), pl.BlockSpec(memory_space=pltpu.VMEM)
    return pl.pallas_call(
        merge_kernel,
        in_specs=[smem, smem, smem, vmem, vmem, vmem, vmem],
        out_specs=pl.BlockSpec(memory_space=pl.ANY),
        out_shape=jax.ShapeDtypeStruct((2, ROWS, FF), jnp.bfloat16),
        scratch_shapes=[
            pltpu.VMEM((2 * ROWS, 2 * TILE), jnp.bfloat16),
            pltpu.VMEM((2 * ROWS, 2 * TILE), jnp.bfloat16),
            pltpu.VMEM((PAIRS // wide, 2, ROWS, wide * TILE), jnp.bfloat16),
            pltpu.SemaphoreType.DMA((PAIRS // wide,)),
        ],
        compiler_params=pltpu.CompilerParams(vmem_limit_bytes=24 * 2**20),
        cost_estimate=pl.CostEstimate(flops=700_000_000, bytes_accessed=4_000_000, transcendentals=0),
    )(order, flags, place, tiles, *ups)


def spread(own):
    swap = [(0, 1), (1, 0)]
    far = lax.ppermute(own, "y", [(y, y ^ 4) for y in range(8)])
    both = jnp.concatenate([own, lax.ppermute(own, "core", swap)], axis=1)
    near = []
    for j in (1, 2, 3):
        pairs = [(2 * y + c, 2 * (y ^ (j + 4 * c)) + c) for y in range(8) for c in range(2)]
        near.append(lax.ppermute(both, ("y", "core"), pairs))
    mine = jnp.concatenate(near + [far], axis=1)
    return both, mine, lax.ppermute(mine, "core", swap)


def body(base_weights, factor_down, factor_up, presence, serving_order):
    place = jnp.stack([lax.axis_index("row"), lax.axis_index("y"), lax.axis_index("core")]).astype(jnp.int32)
    exchange = functools.partial(lax.all_to_all, split_axis=0, concat_axis=0, tiled=True)
    ups = exchange(order_up(serving_order, factor_up).reshape(64, 4, TILE), ("row", "xh"))
    sent = pack(serving_order, base_weights, jnp.swapaxes(factor_down, 1, 2))
    tiles = exchange(sent, "row")
    return merge(serving_order, presence.reshape(-1), place, tiles, spread(ups.reshape(PAIRS, 16, TILE)))


def solution(mesh):
    fine = Mesh(mesh.devices.reshape(16, 8, 4, 2), ("row", "y", "xh", "core"))
    col = ("y", "xh", "core")
    return jax.shard_map(
        body,
        mesh=fine,
        in_specs=(P(None, col, "row"), P(None, col, "row"), P(None, col, "row"), P(), P()),
        out_specs=P("row", col, None),
        check_vma=False,
    )
```

```python
import functools

import jax
import jax.numpy as jnp
from jax import lax
from jax.experimental import pallas as pl
from jax.experimental.pallas import tpu as pltpu
from jax.sharding import Mesh, PartitionSpec as P

TOP = 32767.0
BASE_MAX = 6.0
DOWN_MAX = 6.0
UP_MAX = 0.5
PAIRS = 16
ROWS = 112
TILE = 128
RANKS = 8
FF = 2048
PACKED = 2 * ROWS + 16
CODE = ROWS
DOT = functools.partial(jnp.dot, preferred_element_type=jnp.float32)


def code_of(most, bound):
    root = jnp.sqrt(jnp.sqrt(most * (1.0 / bound)))
    return jnp.clip(jnp.ceil(root * TOP), 1.0, TOP)


def scale_of(code, bound):
    part = code * (1.0 / TOP)
    part = part * part
    return part * part * bound


def signed(root, values):
    root = jnp.minimum(jnp.round(root * TOP), TOP)
    return jnp.where(values < 0.0, -root, root)


def to16(values):
    return values.astype(jnp.int32).astype(jnp.int16)


def halves(values):
    high = values.astype(jnp.bfloat16)
    return high, (values - high.astype(jnp.float32)).astype(jnp.bfloat16)


def order_up_kernel(order_ref, up_ref, out_ref):
    for p in range(PAIRS):
        rows = jnp.concatenate([up_ref[order_ref[2 * p]], up_ref[order_ref[2 * p + 1]]] * 2, axis=0)
        root = jnp.sqrt(jnp.sqrt(jnp.abs(rows) * (1.0 / UP_MAX)))
        out_ref[p] = to16(jnp.concatenate([signed(root, rows)] * 2, axis=0))


def order_up(order, up):
    return pl.pallas_call(
        order_up_kernel,
        in_specs=[pl.BlockSpec(memory_space=pltpu.SMEM), pl.BlockSpec(memory_space=pltpu.VMEM)],
        out_specs=pl.BlockSpec(memory_space=pltpu.VMEM),
        out_shape=jax.ShapeDtypeStruct((PAIRS, 16, TILE), jnp.int16),
        compiler_params=pltpu.CompilerParams(vmem_limit_bytes=60 * 2**20),
        cost_estimate=pl.CostEstimate(flops=0, bytes_accessed=300_000, transcendentals=0),
    )(order, up)


def rooted(part):
    return jnp.round(part * lax.rsqrt(jnp.maximum(jnp.abs(part), 1e-30)) * TOP)


def pack_kernel(per, order_ref, base_ref, down_ref, out_ref):
    first = pl.program_id(0) * per
    row8 = lax.broadcasted_iota(jnp.int32, (8, TILE), 0)
    lane = lax.broadcasted_iota(jnp.int32, (8, TILE), 1)
    experts = [order_ref[first * 2 + i] for i in range(2 * per)]
    low = (row8 & 2) == 0
    for h in range(0, 2 * per, 8):
        most = [jnp.max(jnp.abs(base_ref[e]), axis=0, keepdims=True) for e in experts[h : h + 8]]
        most = jnp.max(jnp.concatenate(most, axis=0), axis=1, keepdims=True)
        codes = code_of(jnp.broadcast_to(most, (8, TILE)), BASE_MAX)
        inverse = 1.0 / scale_of(codes, BASE_MAX)
        most = [jnp.max(jnp.abs(down_ref[e]), axis=1, keepdims=True) for e in experts[h : h + 8]]
        most = jnp.concatenate([jnp.broadcast_to(m, (RANKS, TILE)) for m in most], axis=0)
        down_codes = code_of(most, DOWN_MAX)
        wide = [jnp.concatenate([down_ref[e], jnp.zeros((RANKS, TILE - ROWS), jnp.float32)], axis=1) for e in experts[h : h + 8]]
        downs = rooted(jnp.concatenate(wide, axis=0) * (1.0 / scale_of(down_codes, DOWN_MAX)))
        lanes = lax.broadcasted_iota(jnp.int32, downs.shape, 1)
        downs = jnp.where(lanes < CODE, downs, down_codes)
        for i in range(8):
            p, e = (h + i) // 2, i % 2
            out_ref[p, e * ROWS : (e + 1) * ROWS, :] = to16(rooted(base_ref[experts[h + i]] * inverse[i : i + 1, :]))
        for i in range(0, 8, 2):
            even, odd = downs[8 * i : 8 * i + 8], downs[8 * i + 8 : 8 * i + 16]
            own = jnp.where(low, even, pltpu.roll(odd, 2, 0))
            other = jnp.where(low, pltpu.roll(even, 6, 0), odd)
            rows = []
            for part in (own, other):
                part = jnp.where(lane == CODE + 1, codes[i : i + 1, :], part)
                rows.append(jnp.where(lane == CODE + 2, codes[i + 1 : i + 2, :], part))
            out_ref[(h + i) // 2, 2 * ROWS : PACKED, :] = to16(jnp.concatenate(rows, axis=0))


def pack(order, base, down):
    per = 8
    return pl.pallas_call(
        functools.partial(pack_kernel, per),
        grid_spec=pltpu.PrefetchScalarGridSpec(
            num_scalar_prefetch=1,
            grid=(PAIRS // per,),
            in_specs=[
                pl.BlockSpec(base.shape, lambda i, o: (0, 0, 0)),
                pl.BlockSpec(down.shape, lambda i, o: (0, 0, 0)),
            ],
            out_specs=pl.BlockSpec((per, PACKED, TILE), lambda i, o: (i, 0, 0)),
        ),
        out_shape=jax.ShapeDtypeStruct((PAIRS, PACKED, TILE), jnp.int16),
        compiler_params=pltpu.CompilerParams(vmem_limit_bytes=60 * 2**20),
        cost_estimate=pl.CostEstimate(flops=4_000_000, bytes_accessed=3_000_000, transcendentals=0),
    )(order, base, down)


def sorted_rows(rows, y):
    i = lax.broadcasted_iota(jnp.int32, (2 * TILE, 2 * TILE), 0)
    j = lax.broadcasted_iota(jnp.int32, (2 * TILE, 2 * TILE), 1)
    taker = jnp.where(i < 144, 0, 1)
    at = jnp.where(i < 32, i, jnp.where(i < 144, i - 32, i - 144))
    single = at >= 96
    turn = at >> 5
    apart = jnp.where(i < 32, 0, jnp.where(single, 1, jnp.where(taker == 0, 2 + turn, 7 - turn)))
    of = jnp.where(single, taker, (at >> 4) & 1)
    pick = jnp.where(j == ((of << 7) | ((y ^ apart) << 4) | (i & 15)), 1.0, 0.0).astype(jnp.bfloat16)
    high, low = halves(rows)
    return DOT(pick, high) + DOT(pick, low)


def merge_kernel(order_ref, flag_ref, place_ref, tile_ref, both_ref, fetched_ref, out_ref, left_hi, left_lo, done, sent):
    row, y = place_ref[0], place_ref[1]
    rows = tile_ref[:, 2 * ROWS : PACKED, :].astype(jnp.float32)
    rows = jnp.concatenate([rows[:, 0:8, :].reshape(TILE, TILE), rows[:, 8:16, :].reshape(TILE, TILE)], axis=0)
    factor = sorted_rows(rows, y)
    scale = scale_of(factor[:, CODE : CODE + 1], DOWN_MAX) * (UP_MAX / TOP**2)
    factor = factor * jnp.abs(factor) * scale
    expert = (lax.broadcasted_iota(jnp.int32, (2 * TILE, TILE), 0) >> 1) & 1
    for e in range(2):
        flag = flag_ref[order_ref[2 * row + e]].astype(jnp.float32)
        part = jnp.where(expert == e, factor * flag, 0.0).T[0:ROWS, :]
        at = slice(e * ROWS, (e + 1) * ROWS)
        left_hi[at, :], left_lo[at, :] = halves(part)

    wide = 4
    for i in range(PAIRS // wide):
        spots = range(i * wide, (i + 1) * wide)
        ups = jnp.concatenate([jnp.concatenate([both_ref[s], fetched_ref[s]], axis=0) for s in spots], axis=1)
        ups = ups.astype(jnp.float32) * (1.0 / TOP)
        square = ups * ups
        high, low = halves(square * (ups * jnp.abs(ups)))
        delta = DOT(left_hi[...], high) + (DOT(left_lo[...], high) + DOT(left_hi[...], low))
        for at, s in enumerate(spots):
            codes = tile_ref[s, 2 * ROWS : PACKED, :].astype(jnp.float32)
            for e in range(2):
                scale = scale_of(codes[0:1, CODE + 1 + e : CODE + 2 + e], BASE_MAX) * (1.0 / TOP**2)
                base = tile_ref[s, e * ROWS : (e + 1) * ROWS, :].astype(jnp.float32)
                total = base * jnp.abs(base) * scale + delta[e * ROWS : (e + 1) * ROWS, at * TILE : (at + 1) * TILE]
                done[i, e, :, at * TILE : (at + 1) * TILE] = total.astype(jnp.bfloat16)
        pltpu.make_async_copy(done.at[i], out_ref.at[:, :, pl.ds(i * wide * TILE, wide * TILE)], sent.at[i]).start()
    for i in range(PAIRS // wide):
        pltpu.make_async_copy(done.at[i], out_ref.at[:, :, pl.ds(i * wide * TILE, wide * TILE)], sent.at[i]).wait()


def merge(order, flags, place, tiles, ups):
    wide = 4
    smem, vmem = pl.BlockSpec(memory_space=pltpu.SMEM), pl.BlockSpec(memory_space=pltpu.VMEM)
    return pl.pallas_call(
        merge_kernel,
        in_specs=[smem, smem, smem, vmem, vmem, vmem],
        out_specs=pl.BlockSpec(memory_space=pl.ANY),
        out_shape=jax.ShapeDtypeStruct((2, ROWS, FF), jnp.bfloat16),
        scratch_shapes=[
            pltpu.VMEM((2 * ROWS, 2 * TILE), jnp.bfloat16),
            pltpu.VMEM((2 * ROWS, 2 * TILE), jnp.bfloat16),
            pltpu.VMEM((PAIRS // wide, 2, ROWS, wide * TILE), jnp.bfloat16),
            pltpu.SemaphoreType.DMA((PAIRS // wide,)),
        ],
        compiler_params=pltpu.CompilerParams(vmem_limit_bytes=24 * 2**20),
        cost_estimate=pl.CostEstimate(flops=700_000_000, bytes_accessed=4_000_000, transcendentals=0),
    )(order, flags, place, tiles, *ups)


def spread(own):
    next_to = lax.ppermute(own, "y", [(y, y ^ 1) for y in range(8)])
    both = lax.all_gather(own, "core", axis=1, tiled=True)
    mine = []
    for turn in range(3):
        apart = (2 + turn, 7 - turn)
        pairs = [(2 * y + c, 2 * (y ^ apart[c]) + c) for y in range(8) for c in range(2)]
        mine.append(lax.ppermute(both, ("y", "core"), pairs))
    mine = jnp.concatenate(mine + [next_to], axis=1)
    return both, lax.all_gather(mine, "core", axis=1, tiled=True)


def body(base_weights, factor_down, factor_up, presence, serving_order):
    place = jnp.stack([lax.axis_index("row"), lax.axis_index("y")]).astype(jnp.int32)
    exchange = functools.partial(lax.all_to_all, split_axis=0, concat_axis=0, tiled=True)
    ups = exchange(order_up(serving_order, factor_up).reshape(64, 4, TILE), ("row", "xh"))
    sent = pack(serving_order, base_weights, jnp.swapaxes(factor_down, 1, 2))
    tiles = exchange(sent, "row")
    return merge(serving_order, presence.reshape(-1), place, tiles, spread(ups.reshape(PAIRS, 16, TILE)))


def solution(mesh):
    fine = Mesh(mesh.devices.reshape(16, 8, 4, 2), ("row", "y", "xh", "core"))
    col = ("y", "xh", "core")
    return jax.shard_map(
        body,
        mesh=fine,
        in_specs=(P(None, col, "row"), P(None, col, "row"), P(None, col, "row"), P(), P()),
        out_specs=P("row", col, None),
        check_vma=False,
    )
```

```python
import functools

import jax
import jax.numpy as jnp
from jax import lax
from jax.experimental import pallas as pl
from jax.experimental.pallas import tpu as pltpu
from jax.sharding import Mesh, PartitionSpec as P

TOP = 32767.0
BASE_MAX = 6.0
DOWN_MAX = 6.0
UP_MAX = 0.5
PAIRS = 16
ROWS = 112
TILE = 128
RANKS = 8
FF = 2048
PACKED = 2 * ROWS + 16
CODE = ROWS
DOT = functools.partial(jnp.dot, preferred_element_type=jnp.float32)


def code_of(most, bound):
    root = jnp.sqrt(jnp.sqrt(most * (1.0 / bound)))
    return jnp.clip(jnp.ceil(root * TOP), 1.0, TOP)


def scale_of(code, bound):
    part = code * (1.0 / TOP)
    part = part * part
    return part * part * bound


def signed(root, values):
    root = jnp.minimum(jnp.round(root * TOP), TOP)
    return jnp.where(values < 0.0, -root, root)


def to16(values):
    return values.astype(jnp.int32).astype(jnp.int16)


def halves(values):
    high = values.astype(jnp.bfloat16)
    return high, (values - high.astype(jnp.float32)).astype(jnp.bfloat16)


def order_up_kernel(order_ref, up_ref, out_ref):
    for p in range(PAIRS):
        rows = jnp.concatenate([up_ref[order_ref[2 * p]], up_ref[order_ref[2 * p + 1]]] * 2, axis=0)
        root = jnp.sqrt(jnp.sqrt(jnp.abs(rows) * (1.0 / UP_MAX)))
        out_ref[p] = to16(jnp.concatenate([signed(root, rows)] * 2, axis=0))


def order_up(order, up):
    return pl.pallas_call(
        order_up_kernel,
        in_specs=[pl.BlockSpec(memory_space=pltpu.SMEM), pl.BlockSpec(memory_space=pltpu.VMEM)],
        out_specs=pl.BlockSpec(memory_space=pltpu.VMEM),
        out_shape=jax.ShapeDtypeStruct((PAIRS, 16, TILE), jnp.int16),
        compiler_params=pltpu.CompilerParams(vmem_limit_bytes=60 * 2**20),
        cost_estimate=pl.CostEstimate(flops=0, bytes_accessed=300_000, transcendentals=0),
    )(order, up)


def rooted(part):
    return jnp.round(part * lax.rsqrt(jnp.maximum(jnp.abs(part), 1e-30)) * TOP)


def pack_kernel(per, order_ref, flag_ref, base_ref, down_ref, out_ref):
    first = pl.program_id(0) * per
    row8 = lax.broadcasted_iota(jnp.int32, (8, TILE), 0)
    lane = lax.broadcasted_iota(jnp.int32, (8, TILE), 1)
    experts = [order_ref[first * 2 + i] for i in range(2 * per)]
    low = (row8 & 2) == 0
    for h in range(0, 2 * per, 8):
        most = [jnp.max(jnp.abs(base_ref[e]), axis=0, keepdims=True) for e in experts[h : h + 8]]
        most = jnp.max(jnp.concatenate(most, axis=0), axis=1, keepdims=True)
        codes = code_of(jnp.broadcast_to(most, (8, TILE)), BASE_MAX)
        inverse = 1.0 / scale_of(codes, BASE_MAX)
        most = [jnp.max(jnp.abs(down_ref[e]), axis=1, keepdims=True) for e in experts[h : h + 8]]
        most = jnp.concatenate([jnp.broadcast_to(m, (RANKS, TILE)) for m in most], axis=0)
        down_codes = code_of(most, DOWN_MAX)
        flags = [flag_ref[e >> 4, e & 15].astype(jnp.float32) for e in experts[h : h + 8]]
        wide = [jnp.concatenate([down_ref[e] * f, jnp.zeros((RANKS, TILE - ROWS), jnp.float32)], axis=1) for e, f in zip(experts[h : h + 8], flags)]
        downs = rooted(jnp.concatenate(wide, axis=0) * (1.0 / scale_of(down_codes, DOWN_MAX)))
        lanes = lax.broadcasted_iota(jnp.int32, downs.shape, 1)
        downs = jnp.where(lanes < CODE, downs, down_codes)
        for i in range(8):
            p, e = (h + i) // 2, i % 2
            out_ref[p, e * ROWS : (e + 1) * ROWS, :] = to16(rooted(base_ref[experts[h + i]] * inverse[i : i + 1, :]))
        for i in range(0, 8, 2):
            even, odd = downs[8 * i : 8 * i + 8], downs[8 * i + 8 : 8 * i + 16]
            own = jnp.where(low, even, pltpu.roll(odd, 2, 0))
            other = jnp.where(low, pltpu.roll(even, 6, 0), odd)
            rows = []
            for part in (own, other):
                part = jnp.where(lane == CODE + 1, codes[i : i + 1, :], part)
                rows.append(jnp.where(lane == CODE + 2, codes[i + 1 : i + 2, :], part))
            out_ref[(h + i) // 2, 2 * ROWS : PACKED, :] = to16(jnp.concatenate(rows, axis=0))


def pack(order, flags, base, down):
    per = 8
    return pl.pallas_call(
        functools.partial(pack_kernel, per),
        grid_spec=pltpu.PrefetchScalarGridSpec(
            num_scalar_prefetch=2,
            grid=(PAIRS // per,),
            in_specs=[
                pl.BlockSpec(base.shape, lambda i, *_: (0, 0, 0)),
                pl.BlockSpec(down.shape, lambda i, *_: (0, 0, 0)),
            ],
            out_specs=pl.BlockSpec((per, PACKED, TILE), lambda i, *_: (i, 0, 0)),
        ),
        out_shape=jax.ShapeDtypeStruct((PAIRS, PACKED, TILE), jnp.int16),
        compiler_params=pltpu.CompilerParams(vmem_limit_bytes=60 * 2**20),
        cost_estimate=pl.CostEstimate(flops=4_000_000, bytes_accessed=3_000_000, transcendentals=0),
    )(order, flags, base, down)


def sorter(y):
    i = lax.broadcasted_iota(jnp.int32, (2 * TILE, 2 * TILE), 0)
    j = lax.broadcasted_iota(jnp.int32, (2 * TILE, 2 * TILE), 1)
    taker = jnp.where(i < 144, 0, 1)
    at = jnp.where(i < 32, i, jnp.where(i < 144, i - 32, i - 144))
    single = at >= 96
    turn = at >> 5
    apart = jnp.where(i < 32, 0, jnp.where(single, 1, jnp.where(taker == 0, 2 + turn, 7 - turn)))
    of = jnp.where(single, taker, (at >> 4) & 1)
    return jnp.where(j == ((of << 7) | ((y ^ apart) << 4) | (i & 15)), 1.0, 0.0).astype(jnp.bfloat16)


def merge_kernel(pick_ref, tile_ref, both_ref, fetched_ref, out_ref, left_hi, left_lo, done, sent):
    rows = tile_ref[:, 2 * ROWS : PACKED, :].astype(jnp.float32)
    rows = jnp.concatenate([rows[:, 0:8, :].reshape(TILE, TILE), rows[:, 8:16, :].reshape(TILE, TILE)], axis=0)
    high, low = halves(rows)
    factor = DOT(pick_ref[...], high) + DOT(pick_ref[...], low)
    scale = scale_of(factor[:, CODE : CODE + 1], DOWN_MAX) * (UP_MAX / TOP**2)
    factor = factor * jnp.abs(factor) * scale
    expert = (lax.broadcasted_iota(jnp.int32, (2 * TILE, TILE), 0) >> 1) & 1
    for e in range(2):
        part = jnp.where(expert == e, factor, 0.0).T[0:ROWS, :]
        at = slice(e * ROWS, (e + 1) * ROWS)
        left_hi[at, :], left_lo[at, :] = halves(part)

    wide = 4
    for i in range(PAIRS // wide):
        spots = range(i * wide, (i + 1) * wide)
        ups = jnp.concatenate([jnp.concatenate([both_ref[s], fetched_ref[s]], axis=0) for s in spots], axis=1)
        ups = ups.astype(jnp.float32) * (1.0 / TOP)
        square = ups * ups
        high, low = halves(square * (ups * jnp.abs(ups)))
        delta = DOT(left_hi[...], high) + (DOT(left_lo[...], high) + DOT(left_hi[...], low))
        for at, s in enumerate(spots):
            codes = tile_ref[s, 2 * ROWS : PACKED, :].astype(jnp.float32)
            for e in range(2):
                scale = scale_of(codes[0:1, CODE + 1 + e : CODE + 2 + e], BASE_MAX) * (1.0 / TOP**2)
                base = tile_ref[s, e * ROWS : (e + 1) * ROWS, :].astype(jnp.float32)
                total = base * jnp.abs(base) * scale + delta[e * ROWS : (e + 1) * ROWS, at * TILE : (at + 1) * TILE]
                done[i, e, :, at * TILE : (at + 1) * TILE] = total.astype(jnp.bfloat16)
        pltpu.make_async_copy(done.at[i], out_ref.at[:, :, pl.ds(i * wide * TILE, wide * TILE)], sent.at[i]).start()
    for i in range(PAIRS // wide):
        pltpu.make_async_copy(done.at[i], out_ref.at[:, :, pl.ds(i * wide * TILE, wide * TILE)], sent.at[i]).wait()


def merge(pick, tiles, ups):
    wide = 4
    return pl.pallas_call(
        merge_kernel,
        in_specs=[pl.BlockSpec(memory_space=pltpu.VMEM)] * 4,
        out_specs=pl.BlockSpec(memory_space=pl.ANY),
        out_shape=jax.ShapeDtypeStruct((2, ROWS, FF), jnp.bfloat16),
        scratch_shapes=[
            pltpu.VMEM((2 * ROWS, 2 * TILE), jnp.bfloat16),
            pltpu.VMEM((2 * ROWS, 2 * TILE), jnp.bfloat16),
            pltpu.VMEM((PAIRS // wide, 2, ROWS, wide * TILE), jnp.bfloat16),
            pltpu.SemaphoreType.DMA((PAIRS // wide,)),
        ],
        compiler_params=pltpu.CompilerParams(vmem_limit_bytes=24 * 2**20),
        cost_estimate=pl.CostEstimate(flops=700_000_000, bytes_accessed=4_000_000, transcendentals=0),
    )(pick, tiles, *ups)


def spread(own):
    next_to = lax.ppermute(own, "y", [(y, y ^ 1) for y in range(8)])
    both = lax.all_gather(own, "core", axis=1, tiled=True)
    mine = []
    for turn in range(3):
        apart = (2 + turn, 7 - turn)
        pairs = [(2 * y + c, 2 * (y ^ apart[c]) + c) for y in range(8) for c in range(2)]
        mine.append(lax.ppermute(both, ("y", "core"), pairs))
    mine = jnp.concatenate(mine + [next_to], axis=1)
    return both, lax.all_gather(mine, "core", axis=1, tiled=True)


def body(base_weights, factor_down, factor_up, presence, serving_order):
    exchange = functools.partial(lax.all_to_all, split_axis=0, concat_axis=0, tiled=True)
    ups = exchange(order_up(serving_order, factor_up).reshape(64, 4, TILE), ("row", "xh"))
    sent = pack(serving_order, presence, base_weights, jnp.swapaxes(factor_down, 1, 2))
    tiles = exchange(sent, "row")
    return merge(sorter(lax.axis_index("y")), tiles, spread(ups.reshape(PAIRS, 16, TILE)))


def solution(mesh):
    fine = Mesh(mesh.devices.reshape(16, 8, 4, 2), ("row", "y", "xh", "core"))
    col = ("y", "xh", "core")
    return jax.shard_map(
        body,
        mesh=fine,
        in_specs=(P(None, col, "row"), P(None, col, "row"), P(None, col, "row"), P(), P()),
        out_specs=P("row", col, None),
        check_vma=False,
    )
```
